512 devices in a mesh: ctx: 32 (over z, x_lo, core), head: 16 (over x_hi, y).
Axes of the slice: x: 4 (x_hi: 2, x_lo: 2; x = x_hi * 2 + x_lo), y: 8, z: 8, core: 2. Of those that a mesh axis runs over, the one named last changes fastest.
Arguments:
- q_latent: bfloat16 [4096, 1536], P('ctx', 'head'), may hold values from -72 to 72
- latent_cache: bfloat16 [4096, 576], P('ctx'), may hold values from -6 to 6
- w_q_up: bfloat16 [1536, 12288], P(None, 'head'), may hold values from -0.15625 to 0.15625
- w_kv_up: bfloat16 [512, 16384], P(None, 'head'), may hold values from -0.25 to 0.25
- w_out: bfloat16 [8192, 7168], P('head', 'ctx'), may hold values from -0.5 to 0.5
- token_pos: int32 [4096], P('ctx'), may hold values from 0 to 4095, as said below
- start_offset: int32 [1], replicated, may hold values from 0 to 65535
Outputs:
- layer_out: bfloat16 [4096, 7168], P('ctx', 'head')
The draws below stay inside these ranges and needn't reach their ends.
Inputs may be any that keep to these rules, and one draw needn't show every extreme that they name: `token_pos`: a permutation of 0 to 4095; the 128 tokens of each index of ctx hold consecutive positions in increasing order.
All inputs are finite; a program needn't handle non-finite values.
Results may differ from the reference program's by a relative error of at most 0.035.
Values may be sent and summed in bfloat16 or wider, within the bound.
No kernel may reach another device: no remote copies, remote signals or barrier semaphores. Data moves between devices by JAX's collectives and lax.ppermute only.
A program may use at most 64 MiB of HBM per device.

```python
import jax
import jax.numpy as jnp
from jax import lax

D = 7168
QL = 1536
KVL = 512
NOPE = 128
ROPE = 64
VDIM = 128
HEAD_DEV = 4
TOK_DEV = 128
HEADS = 64
TOKENS = 4096
N_HEAD = 16


def draw_q_latent(key, part):
    first = jax.random.fold_in(key, 0)
    values = jax.random.truncated_normal(first, -6.0, 6.0, (TOKENS, QL), jnp.float32)
    return values.astype(jnp.bfloat16)


def draw_token_pos(key, part):
    blocks = TOKENS // TOK_DEV
    order = jax.random.permutation(key, blocks).astype(jnp.int32)
    inside = jnp.arange(TOK_DEV, dtype=jnp.int32)
    return (order[:, None] * TOK_DEV + inside[None, :]).reshape(TOKENS)


def steps_of(stream_key, shape, pieces, least, top_value):
    factor_of = 1.0
    for position, blocks in pieces:
        steps = jax.random.uniform(jax.random.fold_in(jax.random.fold_in(stream_key, 6), position), (blocks,), jnp.float32, least / len(pieces), top_value / len(pieces))
        factor_of = factor_of * jnp.repeat(jnp.exp(steps), shape[position] // blocks).reshape((-1,) + (1,) * (len(shape) - 1 - position))
    return factor_of


def bell_draw(rng, dims, deviation, bound, cuts=(), kind=jnp.bfloat16):
    array = jax.random.normal(rng, dims, jnp.float32) * deviation
    if len(cuts) > 0:
        array = steps_of(rng, dims, cuts, -0.22, 0.18) * array
    return jnp.clip(array, min=-bound, max=bound).astype(kind)


def setup_inputs(seed: int = 0) -> dict:
    key_of = jax.random.split(jax.random.key(seed), 8)
    q_latent = draw_q_latent(jax.random.fold_in(key_of[7], 71), 0)
    latent_cache = bell_draw(key_of[1], (TOKENS, KVL + ROPE), 1.0, 6.0, ((0, 32),))
    w_q_up = bell_draw(key_of[2], (QL, HEADS * (NOPE + ROPE)), QL ** -0.5, 0.15625, ((1, 16),))
    w_kv_up = bell_draw(key_of[3], (KVL, HEADS * (NOPE + VDIM)), KVL ** -0.5, 0.25, ((1, 16),))
    w_out = bell_draw(key_of[4], (HEADS * VDIM, D), (HEADS * VDIM // 64) ** -0.5, 0.5, ((0, 16), (1, 32)))
    token_pos = draw_token_pos(jax.random.fold_in(key_of[7], 71), 0)
    start_offset = jax.random.randint(key_of[6], (1,), 0, 65536).astype(jnp.int32)
    return {"q_latent": q_latent, "latent_cache": latent_cache, "w_q_up": w_q_up, "w_kv_up": w_kv_up, "w_out": w_out, "token_pos": token_pos, "start_offset": start_offset}


negative_fill = -1e30
softmax_scale = 0.135
rope_base = 10000.0


def rotate(values, angle):
    half = ROPE // 2
    cosine = jnp.cos(angle)
    sine = jnp.sin(angle)
    first = values[..., :half]
    second = values[..., half:]
    return jnp.concatenate([first * cosine - second * sine, first * sine + second * cosine], axis=-1)


def reference(q_latent, latent_cache, w_q_up, w_kv_up, w_out, token_pos, start_offset):
    head_count = HEAD_DEV * N_HEAD
    query = jnp.dot(q_latent, w_q_up, preferred_element_type=jnp.float32).reshape(TOKENS, head_count, NOPE + ROPE)
    absolute = (token_pos + start_offset[0]).astype(jnp.float32)
    freqs = rope_base ** (-jnp.arange(ROPE // 2, dtype=jnp.float32) * 2.0 / ROPE)
    angle = absolute[:, None, None] * freqs[None, None, :]
    query_nope = query[..., :NOPE].astype(jnp.bfloat16)
    query_rope = rotate(query[..., NOPE:], angle).astype(jnp.bfloat16)
    latent = latent_cache[:, :KVL]
    key_rope = latent_cache[:, KVL:]
    visible = token_pos[None, :] <= token_pos[:, None]

    def one_head(index):
        columns = lax.dynamic_slice_in_dim(w_kv_up, (index * (NOPE + VDIM)).astype(jnp.int32), NOPE + VDIM, 1)
        expanded = jnp.dot(latent, columns, preferred_element_type=jnp.float32).astype(jnp.bfloat16)
        head_nope = lax.dynamic_index_in_dim(query_nope, index, 1, keepdims=False)
        head_rope = lax.dynamic_index_in_dim(query_rope, index, 1, keepdims=False)
        scores = jnp.dot(head_nope, expanded[:, :NOPE].T, preferred_element_type=jnp.float32)
        scores = scores + jnp.dot(head_rope, key_rope.T, preferred_element_type=jnp.float32)
        scores = jnp.where(visible, scores * softmax_scale, negative_fill)
        largest = jnp.max(scores, axis=-1, keepdims=True)
        weights = jnp.where(visible, jnp.exp(scores - largest), 0.0)
        totals = jnp.sum(weights, axis=-1, keepdims=True)
        summed = jnp.dot(weights.astype(jnp.bfloat16), expanded[:, NOPE:], preferred_element_type=jnp.float32)
        return (summed / totals).astype(jnp.bfloat16)

    per_head = lax.map(one_head, jnp.arange(head_count, dtype=jnp.int32))
    attention = jnp.transpose(per_head, (1, 0, 2)).reshape(TOKENS, head_count * VDIM)
    group_width = HEAD_DEV * VDIM

    def one_group(index):
        start = (index * group_width).astype(jnp.int32)
        columns = lax.dynamic_slice_in_dim(attention, start, group_width, 1)
        rows = lax.dynamic_slice_in_dim(w_out, start, group_width, 0)
        return jnp.dot(columns, rows, preferred_element_type=jnp.float32).astype(jnp.bfloat16)

    def add_group(total, index):
        return total + one_group(index).astype(jnp.float32), None

    total, unused = lax.scan(add_group, jnp.zeros((TOKENS, D), jnp.float32), jnp.arange(N_HEAD, dtype=jnp.int32))
    return total.astype(jnp.bfloat16)
```

```python
import jax
import jax.numpy as jnp
from jax import lax
from jax.experimental import pallas as pl
from jax.experimental.pallas import tpu as pltpu
from jax.sharding import Mesh, PartitionSpec as P

QL = 1536
KVL = 512
NOPE = 128
ROPE = 64
VDIM = 128
HEADS = 4
TOK = 128
QD = NOPE + ROPE
KROWS = KVL + ROPE + 16
QROWS = HEADS * QD + 16
OROWS = HEADS * VDIM + 16

softmax_scale = 0.135
rope_base = 10000.0
masked = -1e30
floor = -1e29

F32 = jnp.float32
BF16 = jnp.bfloat16
CTX = ("z", "xl", "core")
NEAR = ("xl", "core")
VMEM = pl.BlockSpec(memory_space=pltpu.VMEM)
LIMIT = 56 * 1024 * 1024


def dot(a, b):
    return jnp.dot(a, b, preferred_element_type=F32)


def kernel_call(body, shape, args, scratch=(), flops=0):
    return pl.pallas_call(
        body,
        out_shape=jax.ShapeDtypeStruct(shape, BF16),
        in_specs=[VMEM] * len(args),
        out_specs=VMEM,
        scratch_shapes=list(scratch),
        compiler_params=pltpu.CompilerParams(vmem_limit_bytes=LIMIT),
        cost_estimate=pl.CostEstimate(flops=flops, bytes_accessed=4_000_000, transcendentals=0),
    )(*args)


def query_body(latent, weights, cosine, sine, pos, out):
    query = dot(weights[...], latent[...])
    cos, sin = cosine[...], sine[...]
    half = ROPE // 2
    for h in range(HEADS):
        base = h * QD
        out[base : base + NOPE, :] = query[base : base + NOPE].astype(BF16)
        a = query[base + NOPE : base + NOPE + half]
        b = query[base + NOPE + half : base + QD]
        out[base + NOPE : base + QD, :] = jnp.concatenate(
            [a * cos - b * sin, a * sin + b * cos], axis=0
        ).astype(BF16)
    out[HEADS * QD :, :] = pos[...]


def attend_body(queries, keys, w_key, w_value_t, out, latent, rope_keys, key_pos, key_cat, value_t):
    blocks = keys.shape[0]
    tokens = queries.shape[0]
    for z in range(blocks):
        rows = slice(z * TOK, (z + 1) * TOK)
        latent[rows, :] = keys[z, :KVL, :].T
        tail = keys[z, KVL:, :].astype(F32).T
        rope_keys[rows, :] = tail[:, :ROPE].astype(BF16)
        key_pos[rows, :] = tail[:, ROPE : ROPE + 1] * 64.0 + tail[:, ROPE + 1 : ROPE + 2]
        value_t[:, rows] = dot(w_value_t[...], keys[z, :KVL, :]).astype(BF16)
    expanded = dot(latent[...], w_key[...]).astype(BF16)
    for h in range(HEADS):
        key_cat[h, :, :NOPE] = expanded[:, h * NOPE : (h + 1) * NOPE]
        key_cat[h, :, NOPE:] = rope_keys[...]
    positions = key_pos[...]
    for pair in range(tokens // 2):
        two = (2 * pair, 2 * pair + 1)
        q_pos = jnp.concatenate(
            [queries[t, HEADS * QD : HEADS * QD + 2, :].astype(F32) for t in two], axis=1
        )
        q_pos = q_pos[0:1] * 64.0 + q_pos[1:2]
        visible = positions <= q_pos
        stats = []
        for h in range(HEADS):
            q = jnp.concatenate([queries[t, h * QD : (h + 1) * QD, :] for t in two], axis=1)
            scores = jnp.where(visible, dot(key_cat[h], q) * softmax_scale, masked)
            largest = jnp.maximum(jnp.max(scores, axis=0, keepdims=True), floor)
            weights = jnp.exp(scores - largest)
            total = jnp.sum(weights, axis=0, keepdims=True)
            some = total > 0.0
            safe = jnp.where(some, total, 1.0)
            summed = dot(value_t[h * VDIM : (h + 1) * VDIM, :], weights.astype(BF16)) / safe
            level = jnp.where(some, largest + jnp.log(safe), masked)
            first = level.astype(BF16)
            rest = level - first.astype(F32)
            second = rest.astype(BF16)
            third = (rest - second.astype(F32)).astype(BF16)
            stats += [first.astype(F32), second.astype(F32), third.astype(F32)]
            summed = summed.astype(BF16)
            for i, t in enumerate(two):
                out[t, h * VDIM : (h + 1) * VDIM, :] = summed[:, i * TOK : (i + 1) * TOK]
        stats = jnp.concatenate(stats + [jnp.zeros_like(stats[0])] * 4, axis=0).astype(BF16)
        for i, t in enumerate(two):
            out[t, HEADS * VDIM :, :] = stats[:, i * TOK : (i + 1) * TOK]


def merge_body(parts, out):
    count = parts.shape[0]
    tails = [parts[s, HEADS * VDIM :, :].astype(F32) for s in range(count)]
    for h in range(HEADS):
        levels = [t[3 * h : 3 * h + 1] + t[3 * h + 1 : 3 * h + 2] + t[3 * h + 2 : 3 * h + 3] for t in tails]
        top = levels[0]
        for level in levels[1:]:
            top = jnp.maximum(top, level)
        shares = [jnp.exp(level - top) for level in levels]
        rows = slice(h * VDIM, (h + 1) * VDIM)
        whole = sum(shares)
        added = sum(parts[s, rows, :].astype(F32) * shares[s] for s in range(count))
        out[rows, :] = (added / whole).astype(BF16)


def project_body(w, x, out):
    out[...] = (dot(w[0], x[0]) + dot(w[1], x[1])).astype(BF16)


def project(w, x, tiles):
    rows = w.shape[1] // tiles
    return pl.pallas_call(
        project_body,
        grid=(tiles,),
        out_shape=jax.ShapeDtypeStruct((w.shape[1], TOK), BF16),
        in_specs=[
            pl.BlockSpec((2, rows, w.shape[2]), lambda i: (0, i, 0)),
            pl.BlockSpec((2, x.shape[1], TOK), lambda i: (0, 0, 0)),
        ],
        out_specs=pl.BlockSpec((rows, TOK), lambda i: (i, 0)),
        compiler_params=pltpu.CompilerParams(vmem_limit_bytes=LIMIT),
        cost_estimate=pl.CostEstimate(
            flops=4 * w.shape[1] * w.shape[2] * TOK, bytes_accessed=8_000_000, transcendentals=0
        ),
    )(w, x)


def sent_to_all(array, axis):
    copies = jnp.broadcast_to(array, (lax.axis_size(axis), *array.shape))
    return lax.all_to_all(copies, axis, split_axis=0, concat_axis=0, tiled=True)


def crossed():
    pairs = []
    for z in range(8):
        for xh in range(2):
            source = z * 2 + xh
            target = source if z // 4 == xh else (z ^ 4) * 2 + (1 - xh)
            pairs.append((source, target))
    return pairs


def shards(q_latent, latent_cache, w_q_up, w_kv_up, w_out, token_pos, start_offset):
    pos_rows = jnp.concatenate(
        [(token_pos >> 6)[None], (token_pos & 63)[None], jnp.zeros((14, TOK), jnp.int32)], axis=0
    ).astype(BF16)

    w_mine = lax.ppermute(w_out.T, ("z", "xh"), crossed())
    w_all = lax.all_gather(w_mine, CTX, axis=0, tiled=False)

    latent = sent_to_all(q_latent.T, ("xh", "y")).reshape(QL, TOK)
    keys = jnp.concatenate([latent_cache.T, pos_rows], axis=0)
    keys = sent_to_all(keys, "z")

    absolute = (token_pos + start_offset[0]).astype(F32)
    freqs = rope_base ** (-jnp.arange(ROPE // 2, dtype=F32) * 2.0 / ROPE)
    angle = freqs[:, None] * absolute[None, :]
    query = kernel_call(
        query_body,
        (QROWS, TOK),
        (latent, w_q_up.T, jnp.cos(angle), jnp.sin(angle), pos_rows),
        flops=300_000_000,
    )
    queries = lax.all_gather(query, NEAR, axis=0, tiled=False)

    per_head = w_kv_up.reshape(KVL, HEADS, NOPE + VDIM)
    w_key = per_head[:, :, :NOPE].reshape(KVL, HEADS * NOPE)
    w_value_t = per_head[:, :, NOPE:].reshape(KVL, HEADS * VDIM).T
    count = keys.shape[0] * TOK
    parts = kernel_call(
        attend_body,
        (4, OROWS, TOK),
        (queries, keys, w_key, w_value_t),
        scratch=(
            pltpu.VMEM((count, KVL), BF16),
            pltpu.VMEM((count, ROPE), BF16),
            pltpu.VMEM((count, 1), F32),
            pltpu.VMEM((HEADS, count, QD), BF16),
            pltpu.VMEM((HEADS * VDIM, count), BF16),
        ),
        flops=3_500_000_000,
    )
    parts = lax.all_to_all(parts, NEAR, split_axis=0, concat_axis=0, tiled=True)
    mine = kernel_call(merge_body, (HEADS * VDIM, TOK), (parts,), flops=1_000_000)
    both = lax.all_gather(mine, "xh", axis=0, tiled=False)

    w_all = w_all.reshape(2, -1, HEADS * VDIM)
    partial = project(w_all, both, 8)
    partial = partial.reshape(8, -1, TOK)
    arrived = lax.all_to_all(partial, "y", split_axis=0, concat_axis=0, tiled=True)
    return arrived.astype(F32).sum(axis=0).astype(BF16).T


def solution(mesh):
    fine = Mesh(mesh.devices.reshape(8, 2, 2, 2, 8), ("z", "xl", "core", "xh", "y"))
    head = ("xh", "y")
    in_specs = (
        P(CTX, head),
        P(CTX, None),
        P(None, head),
        P(None, head),
        P(head, CTX),
        P(CTX),
        P(),
    )
    return jax.shard_map(
        shards, mesh=fine, in_specs=in_specs, out_specs=P(CTX, head), check_vma=False
    )
```

```python
import itertools

import jax
import jax.numpy as jnp
from jax import lax
from jax.experimental import pallas as pl
from jax.experimental.pallas import tpu as pltpu
from jax.sharding import Mesh, PartitionSpec as P

QL = 1536
KVL = 512
NOPE = 128
ROPE = 64
VDIM = 128
HEADS = 4
TOK = 128
QD = NOPE + ROPE
KROWS = KVL + ROPE + 16
QROWS = HEADS * QD + 16
OROWS = HEADS * VDIM + 16

softmax_scale = 0.135
rope_base = 10000.0
masked = -1e30
floor = -1e29

F32 = jnp.float32
BF16 = jnp.bfloat16
CTX = ("za", "zb", "xl", "core")
NEAR = ("xl", "core")
VMEM = pl.BlockSpec(memory_space=pltpu.VMEM)
LIMIT = 56 * 1024 * 1024


def dot(a, b):
    return jnp.dot(a, b, preferred_element_type=F32)


def kernel_call(body, shape, args, scratch=(), flops=0):
    return pl.pallas_call(
        body,
        out_shape=jax.ShapeDtypeStruct(shape, BF16),
        in_specs=[VMEM] * len(args),
        out_specs=VMEM,
        scratch_shapes=list(scratch),
        compiler_params=pltpu.CompilerParams(vmem_limit_bytes=LIMIT),
        cost_estimate=pl.CostEstimate(flops=flops, bytes_accessed=4_000_000, transcendentals=0),
    )(*args)


def query_body(latent, weights, cosine, sine, pos, out):
    query = dot(weights[...], latent[...])
    cos, sin = cosine[...], sine[...]
    half = ROPE // 2
    for h in range(HEADS):
        base = h * QD
        out[base : base + NOPE, :] = query[base : base + NOPE].astype(BF16)
        a = query[base + NOPE : base + NOPE + half]
        b = query[base + NOPE + half : base + QD]
        out[base + NOPE : base + QD, :] = jnp.concatenate(
            [a * cos - b * sin, a * sin + b * cos], axis=0
        ).astype(BF16)
    out[HEADS * QD :, :] = pos[...]


def attend_body(queries, keys, w_key, w_value_t, out, latent, rope_keys, key_pos, key_cat, value_t):
    blocks = keys.shape[0]
    tokens = queries.shape[0]
    for z in range(blocks):
        rows = slice(z * TOK, (z + 1) * TOK)
        latent[rows, :] = keys[z, :KVL, :].T
        tail = keys[z, KVL:, :].astype(F32).T
        rope_keys[rows, :] = tail[:, :ROPE].astype(BF16)
        key_pos[rows, :] = tail[:, ROPE : ROPE + 1] * 64.0 + tail[:, ROPE + 1 : ROPE + 2]
        value_t[:, rows] = dot(w_value_t[...], keys[z, :KVL, :]).astype(BF16)
    expanded = dot(latent[...], w_key[...]).astype(BF16)
    for h in range(HEADS):
        key_cat[h, :, :NOPE] = expanded[:, h * NOPE : (h + 1) * NOPE]
        key_cat[h, :, NOPE:] = rope_keys[...]
    positions = key_pos[...]
    for pair in range(tokens // 2):
        two = (2 * pair, 2 * pair + 1)
        q_pos = jnp.concatenate(
            [queries[t, HEADS * QD : HEADS * QD + 2, :].astype(F32) for t in two], axis=1
        )
        q_pos = q_pos[0:1] * 64.0 + q_pos[1:2]
        visible = positions <= q_pos
        stats = []
        for h in range(HEADS):
            q = jnp.concatenate([queries[t, h * QD : (h + 1) * QD, :] for t in two], axis=1)
            scores = jnp.where(visible, dot(key_cat[h], q) * softmax_scale, masked)
            largest = jnp.maximum(jnp.max(scores, axis=0, keepdims=True), floor)
            weights = jnp.exp(scores - largest)
            total = jnp.sum(weights, axis=0, keepdims=True)
            some = total > 0.0
            safe = jnp.where(some, total, 1.0)
            summed = dot(value_t[h * VDIM : (h + 1) * VDIM, :], weights.astype(BF16)) / safe
            level = jnp.where(some, largest + jnp.log(safe), masked)
            first = level.astype(BF16)
            rest = level - first.astype(F32)
            second = rest.astype(BF16)
            third = (rest - second.astype(F32)).astype(BF16)
            stats += [first.astype(F32), second.astype(F32), third.astype(F32)]
            summed = summed.astype(BF16)
            for i, t in enumerate(two):
                out[t, h * VDIM : (h + 1) * VDIM, :] = summed[:, i * TOK : (i + 1) * TOK]
        stats = jnp.concatenate(stats + [jnp.zeros_like(stats[0])] * 4, axis=0).astype(BF16)
        for i, t in enumerate(two):
            out[t, HEADS * VDIM :, :] = stats[:, i * TOK : (i + 1) * TOK]


def merge_body(parts, out):
    count = parts.shape[0]
    tails = [parts[s, HEADS * VDIM :, :].astype(F32) for s in range(count)]
    for h in range(HEADS):
        levels = [t[3 * h : 3 * h + 1] + t[3 * h + 1 : 3 * h + 2] + t[3 * h + 2 : 3 * h + 3] for t in tails]
        top = levels[0]
        for level in levels[1:]:
            top = jnp.maximum(top, level)
        shares = [jnp.exp(level - top) for level in levels]
        rows = slice(h * VDIM, (h + 1) * VDIM)
        whole = sum(shares)
        added = sum(parts[s, rows, :].astype(F32) * shares[s] for s in range(count))
        out[rows, :] = (added / whole).astype(BF16)


def project_body(w, mine, theirs, place, out):
    total = 0.0
    rows = w.shape[0] * w.shape[2]
    for g in range(4):
        group = place[0] ^ g
        tokens = jnp.concatenate([mine[group], theirs[group]], axis=1)
        total = total + dot(w[:, g].reshape(rows, w.shape[3]), tokens)
    out[...] = total.astype(BF16).reshape(out.shape)


def project(w, mine, theirs, place):
    tiles, _, rows, depth = w.shape
    wide = 2 * TOK
    return pl.pallas_call(
        project_body,
        grid=(tiles // 2,),
        out_shape=jax.ShapeDtypeStruct((tiles, rows, wide), BF16),
        in_specs=[
            pl.BlockSpec((2, 4, rows, depth), lambda i: (i, 0, 0, 0)),
            pl.BlockSpec(mine.shape, lambda i: (0, 0, 0)),
            pl.BlockSpec(mine.shape, lambda i: (0, 0, 0)),
            pl.BlockSpec(memory_space=pltpu.SMEM),
        ],
        out_specs=pl.BlockSpec((2, rows, wide), lambda i: (i, 0, 0)),
        compiler_params=pltpu.CompilerParams(vmem_limit_bytes=LIMIT),
        cost_estimate=pl.CostEstimate(
            flops=8 * tiles * rows * depth * wide, bytes_accessed=5_000_000, transcendentals=0
        ),
    )(w, mine, theirs, place)


def sent_to_all(array, axis):
    copies = jnp.broadcast_to(array, (lax.axis_size(axis), *array.shape))
    return lax.all_to_all(copies, axis, split_axis=0, concat_axis=0, tiled=True)


def crossed(half, flip):
    pairs = []
    for b, c, d in itertools.product(range(2), repeat=3):
        pairs.append(((b * 2 + c) * 2 + d, ((d ^ flip) * 2 + (c ^ half)) * 2 + b))
    return pairs


def shards(q_latent, latent_cache, w_q_up, w_kv_up, w_out, token_pos, start_offset):
    pos_rows = jnp.concatenate(
        [(token_pos >> 6)[None], (token_pos & 63)[None], jnp.zeros((14, TOK), jnp.int32)], axis=0
    ).astype(BF16)

    columns = w_out.T.reshape(2, -1, HEADS * VDIM)
    xh = lax.axis_index("xh")
    halves = [lax.dynamic_index_in_dim(columns, xh ^ half, 0, keepdims=False) for half in range(2)]
    w_mine = [
        lax.ppermute(halves[half], ("xl", "xh", "yl"), crossed(half, flip))
        for half in range(2)
        for flip in range(2)
    ]
    keys = jnp.concatenate([latent_cache.T, pos_rows], axis=0)
    keys = lax.all_gather(keys, ("za", "zb"), axis=0, tiled=False)
    latent = sent_to_all(q_latent.T, ("xh", "yh", "yl")).reshape(QL, TOK)
    latent, w_mine = lax.optimization_barrier((latent, w_mine))
    w_all = lax.all_gather(jnp.stack(w_mine), ("za", "zb"), axis=0, tiled=False)

    absolute = (token_pos + start_offset[0]).astype(F32)
    freqs = rope_base ** (-jnp.arange(ROPE // 2, dtype=F32) * 2.0 / ROPE)
    angle = freqs[:, None] * absolute[None, :]
    query = kernel_call(
        query_body,
        (QROWS, TOK),
        (latent, w_q_up.T, jnp.cos(angle), jnp.sin(angle), pos_rows),
        flops=300_000_000,
    )
    queries = lax.all_gather(query, NEAR, axis=0, tiled=False)

    per_head = w_kv_up.reshape(KVL, HEADS, NOPE + VDIM)
    w_key = per_head[:, :, :NOPE].reshape(KVL, HEADS * NOPE)
    w_value_t = per_head[:, :, NOPE:].reshape(KVL, HEADS * VDIM).T
    count = keys.shape[0] * TOK
    parts = kernel_call(
        attend_body,
        (4, OROWS, TOK),
        (queries, keys, w_key, w_value_t),
        scratch=(
            pltpu.VMEM((count, KVL), BF16),
            pltpu.VMEM((count, ROPE), BF16),
            pltpu.VMEM((count, 1), F32),
            pltpu.VMEM((HEADS, count, QD), BF16),
            pltpu.VMEM((HEADS * VDIM, count), BF16),
        ),
        flops=3_500_000_000,
    )
    parts = lax.all_to_all(parts, NEAR, split_axis=0, concat_axis=0, tiled=True)
    mine = kernel_call(merge_body, (HEADS * VDIM, TOK), (parts,), flops=1_000_000)
    mine = lax.all_gather(mine, ("xh", "yl"), axis=0, tiled=False)
    theirs = lax.ppermute(mine, "core", [(0, 1), (1, 0)])
    place = (xh * 2 + lax.axis_index("xl")).astype(jnp.int32)[None]
    partial = project(w_all, mine, theirs, place)
    arrived = lax.all_to_all(partial, ("xh", "yh"), split_axis=0, concat_axis=0, tiled=True)
    arrived = arrived.reshape(2, 4, -1, 2 * TOK)
    summed = arrived.astype(F32).sum(axis=1).astype(BF16).reshape(-1, 2 * TOK)
    kept = summed[:, :TOK]
    got = lax.ppermute(summed[:, TOK:], "core", [(0, 1), (1, 0)])
    first = lax.axis_index("core") == 0
    return jnp.concatenate([jnp.where(first, kept, got), jnp.where(first, got, kept)], axis=0).T


def solution(mesh):
    fine = Mesh(mesh.devices.reshape(2, 4, 2, 2, 2, 4, 2), ("za", "zb", "xl", "core", "xh", "yh", "yl"))
    head = ("xh", "yh", "yl")
    in_specs = (
        P(CTX, head),
        P(CTX, None),
        P(None, head),
        P(None, head),
        P(head, CTX),
        P(CTX),
        P(),
    )
    return jax.shard_map(
        shards, mesh=fine, in_specs=in_specs, out_specs=P(CTX, head), check_vma=False
    )
```

```python
import itertools
import math

import jax
import jax.numpy as jnp
from jax import lax
from jax.experimental import pallas as pl
from jax.experimental.pallas import tpu as pltpu
from jax.sharding import Mesh, PartitionSpec as P

QL = 1536
KVL = 512
NOPE = 128
ROPE = 64
VDIM = 128
HEADS = 4
TOK = 128
QD = NOPE + ROPE
KROWS = KVL + ROPE + 16
QROWS = HEADS * QD + 16
OROWS = HEADS * VDIM + 16

softmax_scale = 0.135
scale = softmax_scale * math.log2(math.e)
rope_base = 10000.0
masked = -1e30
floor = -1e29

F32 = jnp.float32
BF16 = jnp.bfloat16
CTX = ("za", "zb", "xl", "core")
NEAR = ("xl", "core")
VMEM = pl.BlockSpec(memory_space=pltpu.VMEM)
LIMIT = 56 * 1024 * 1024


def dot(a, b):
    return jnp.dot(a, b, preferred_element_type=F32)


def kernel_call(body, shapes, args, scratch=(), flops=0, specs=None):
    single = isinstance(shapes, tuple)
    outs = [jax.ShapeDtypeStruct(shape, BF16) for shape in ([shapes] if single else shapes)]
    return pl.pallas_call(
        body,
        out_shape=outs[0] if single else outs,
        in_specs=specs or [VMEM] * len(args),
        out_specs=VMEM if single else [VMEM] * len(outs),
        scratch_shapes=list(scratch),
        compiler_params=pltpu.CompilerParams(vmem_limit_bytes=LIMIT),
        cost_estimate=pl.CostEstimate(flops=flops, bytes_accessed=4_000_000, transcendentals=0),
    )(*args)


def position_rows(pos):
    row = lax.broadcasted_iota(jnp.int32, (16, TOK), 0)
    pos = jnp.broadcast_to(pos, (16, TOK))
    return jnp.where(row == 0, pos >> 6, jnp.where(row == 1, pos & 63, 0)).astype(F32).astype(BF16)


def pack_body(latent, pos, out):
    out[: KVL + ROPE, :] = latent[...]
    out[KVL + ROPE :, :] = position_rows(pos[...])


def weights_body(w, w_key, w_value_t):
    for h in range(HEADS):
        base = h * (NOPE + VDIM)
        cols = slice(h * NOPE, (h + 1) * NOPE)
        w_key[:, cols] = w[:, base : base + NOPE]
        w_value_t[cols, :] = w[:, base + NOPE : base + NOPE + VDIM].T


def query_body(latent, weights, cosine, sine, pos, out):
    query = dot(latent[...].T, weights[...]).T
    cos, sin = cosine[...], sine[...]
    half = ROPE // 2
    for h in range(HEADS):
        base = h * QD
        out[base : base + NOPE, :] = query[base : base + NOPE].astype(BF16)
        a = query[base + NOPE : base + NOPE + half]
        b = query[base + NOPE + half : base + QD]
        out[base + NOPE : base + QD, :] = jnp.concatenate(
            [a * cos - b * sin, a * sin + b * cos], axis=0
        ).astype(BF16)
    out[HEADS * QD :, :] = position_rows(pos[...])


def attend_body(queries, keys, w_key, w_value_t, out, latent, rope_keys, key_pos, key_cat, value_t):
    blocks = keys.shape[0]
    tokens = queries.shape[0]
    for z in range(blocks):
        rows = slice(z * TOK, (z + 1) * TOK)
        latent[rows, :] = keys[z, :KVL, :].T
        tail = keys[z, KVL:, :].astype(F32).T
        rope_keys[rows, :] = tail[:, :ROPE].astype(BF16)
        key_pos[rows, :] = tail[:, ROPE : ROPE + 1] * 64.0 + tail[:, ROPE + 1 : ROPE + 2]
        value_t[:, rows] = dot(w_value_t[...], keys[z, :KVL, :]).astype(BF16)
    expanded = dot(latent[...], w_key[...]).astype(BF16)
    for h in range(HEADS):
        key_cat[h, :, :NOPE] = expanded[:, h * NOPE : (h + 1) * NOPE]
        key_cat[h, :, NOPE:] = rope_keys[...]
    positions = key_pos[...]
    for pair in range(tokens // 2):
        two = (2 * pair, 2 * pair + 1)
        q_pos = jnp.concatenate(
            [queries[t, HEADS * QD : HEADS * QD + 2, :].astype(F32) for t in two], axis=1
        )
        q_pos = q_pos[0:1] * 64.0 + q_pos[1:2]
        visible = positions <= q_pos
        stats = []
        for h in range(HEADS):
            q = jnp.concatenate([queries[t, h * QD : (h + 1) * QD, :] for t in two], axis=1)
            scores = jnp.where(visible, dot(key_cat[h], q) * scale, masked)
            largest = jnp.maximum(jnp.max(scores, axis=0, keepdims=True), floor)
            weights = jnp.exp2(scores - largest)
            total = jnp.sum(weights, axis=0, keepdims=True)
            some = total > 0.0
            safe = jnp.where(some, total, 1.0)
            summed = dot(value_t[h * VDIM : (h + 1) * VDIM, :], weights.astype(BF16)) / safe
            level = jnp.where(some, largest + jnp.log2(safe), masked)
            first = level.astype(BF16)
            rest = level - first.astype(F32)
            second = rest.astype(BF16)
            third = (rest - second.astype(F32)).astype(BF16)
            stats += [first.astype(F32), second.astype(F32), third.astype(F32)]
            summed = summed.astype(BF16)
            for i, t in enumerate(two):
                out[t, h * VDIM : (h + 1) * VDIM, :] = summed[:, i * TOK : (i + 1) * TOK]
        stats = jnp.concatenate(stats + [jnp.zeros_like(stats[0])] * 4, axis=0).astype(BF16)
        for i, t in enumerate(two):
            out[t, HEADS * VDIM :, :] = stats[:, i * TOK : (i + 1) * TOK]


def merge_body(parts, out):
    count = parts.shape[0]
    tails = [parts[s, HEADS * VDIM :, :].astype(F32) for s in range(count)]
    for h in range(HEADS):
        levels = [t[3 * h : 3 * h + 1] + t[3 * h + 1 : 3 * h + 2] + t[3 * h + 2 : 3 * h + 3] for t in tails]
        top = levels[0]
        for level in levels[1:]:
            top = jnp.maximum(top, level)
        shares = [jnp.exp2(level - top) for level in levels]
        rows = slice(h * VDIM, (h + 1) * VDIM)
        whole = sum(shares)
        added = sum(parts[s, rows, :].astype(F32) * shares[s] for s in range(count))
        out[rows, :] = (added / whole).astype(BF16)


def project_body(w, mine, theirs, place, out, total):
    step = pl.program_id(0)
    rows = w.shape[0] * w.shape[2]
    added = 0.0
    for g in range(w.shape[1]):
        group = place[0] ^ (step * w.shape[1] + g)
        tokens = jnp.concatenate([mine[group], theirs[group]], axis=1)
        added = added + dot(w[:, g].reshape(rows, w.shape[3]), tokens)

    @pl.when(step == 0)
    def _():
        total[...] = added

    @pl.when(step > 0)
    def _():
        total[...] += added

    @pl.when(step == pl.num_programs(0) - 1)
    def _():
        here = place[1]
        tile = w.shape[2]
        for z in range(w.shape[0]):
            piece = total[z * tile : (z + 1) * tile, :].astype(BF16)
            out[z % 4, here, z // 4] = piece[:, :TOK]
            out[z % 4, 1 - here, z // 4] = piece[:, TOK:]


def project(w, mine, theirs, place):
    tiles, groups, rows, depth = w.shape
    wide = 2 * TOK
    return pl.pallas_call(
        project_body,
        grid=(groups // 2,),
        out_shape=jax.ShapeDtypeStruct((tiles // 2, 2, 2, rows, TOK), BF16),
        in_specs=[
            pl.BlockSpec((tiles, 2, rows, depth), lambda i: (0, i, 0, 0)),
            pl.BlockSpec(mine.shape, lambda i: (0, 0, 0)),
            pl.BlockSpec(mine.shape, lambda i: (0, 0, 0)),
            pl.BlockSpec(memory_space=pltpu.SMEM),
        ],
        out_specs=pl.BlockSpec((tiles // 2, 2, 2, rows, TOK), lambda i: (0, 0, 0, 0, 0)),
        scratch_shapes=[pltpu.VMEM((tiles * rows, wide), F32)],
        compiler_params=pltpu.CompilerParams(vmem_limit_bytes=LIMIT),
        cost_estimate=pl.CostEstimate(
            flops=2 * groups * tiles * rows * depth * wide, bytes_accessed=5_000_000, transcendentals=0
        ),
    )(w, mine, theirs, place)


def sent_to_all(array, axis):
    copies = jnp.broadcast_to(array, (lax.axis_size(axis), *array.shape))
    return lax.all_to_all(copies, axis, split_axis=0, concat_axis=0, tiled=True)


def crossed(half, flip):
    pairs = []
    for b, c, d in itertools.product(range(2), repeat=3):
        pairs.append(((b * 2 + c) * 2 + d, ((d ^ flip) * 2 + (c ^ half)) * 2 + b))
    return pairs


def shards(q_latent, latent_cache, w_q_up, w_kv_up, w_out, token_pos, start_offset):
    columns = w_out.T.reshape(2, -1, HEADS * VDIM)
    xh = lax.axis_index("xh")
    halves = [lax.dynamic_index_in_dim(columns, xh ^ half, 0, keepdims=False) for half in range(2)]
    w_mine = [
        lax.ppermute(halves[half], ("xl", "xh", "yl"), crossed(half, flip))
        for flip in range(2)
        for half in range(2)
    ]
    keys = kernel_call(pack_body, (KROWS, TOK), (latent_cache.T, token_pos[None]))
    keys = lax.all_gather(keys, ("za", "zb"), axis=0, tiled=False)
    latent = sent_to_all(q_latent.T, ("xh", "yh", "yl")).reshape(QL, TOK)

    absolute = (token_pos + start_offset[0]).astype(F32)
    freqs = rope_base ** (-jnp.arange(ROPE // 2, dtype=F32) * 2.0 / ROPE)
    angle = freqs[:, None] * absolute[None, :]
    query = kernel_call(
        query_body,
        (QROWS, TOK),
        (latent, w_q_up, jnp.cos(angle), jnp.sin(angle), token_pos[None]),
        flops=300_000_000,
    )
    query, w_mine = lax.optimization_barrier((query, w_mine))
    w_all = lax.all_gather(jnp.stack(w_mine), ("za", "zb"), axis=0, tiled=False)
    queries = lax.all_gather(query, NEAR, axis=0, tiled=False)

    w_key, w_value_t = kernel_call(weights_body, [(KVL, HEADS * NOPE), (HEADS * VDIM, KVL)], (w_kv_up,))
    count = keys.shape[0] * TOK
    parts = kernel_call(
        attend_body,
        (4, OROWS, TOK),
        (queries, keys, w_key, w_value_t),
        scratch=(
            pltpu.VMEM((count, KVL), BF16),
            pltpu.VMEM((count, ROPE), BF16),
            pltpu.VMEM((count, 1), F32),
            pltpu.VMEM((HEADS, count, QD), BF16),
            pltpu.VMEM((HEADS * VDIM, count), BF16),
        ),
        flops=3_500_000_000,
    )
    parts = lax.all_to_all(parts, NEAR, split_axis=0, concat_axis=0, tiled=True)
    mine = kernel_call(merge_body, (HEADS * VDIM, TOK), (parts,), flops=1_000_000)
    mine = sent_to_all(mine, ("yl", "xh"))
    theirs = lax.ppermute(mine, "core", [(0, 1), (1, 0)])
    place = jnp.stack([lax.axis_index("xl") * 2 + xh, lax.axis_index("core")]).astype(jnp.int32)
    partial = project(w_all, mine, theirs, place)
    partial = partial.reshape(16, -1, TOK)
    arrived = lax.all_to_all(partial, ("yh", "core", "xh"), split_axis=0, concat_axis=0, tiled=True)
    arrived = arrived.reshape(4, 4, -1, TOK)
    return arrived.astype(F32).sum(axis=0).astype(BF16).reshape(-1, TOK).T


def solution(mesh):
    fine = Mesh(mesh.devices.reshape(2, 4, 2, 2, 2, 4, 2), ("za", "zb", "xl", "core", "xh", "yh", "yl"))
    head = ("xh", "yh", "yl")
    in_specs = (
        P(CTX, head),
        P(CTX, None),
        P(None, head),
        P(None, head),
        P(head, CTX),
        P(CTX),
        P(),
    )
    return jax.shard_map(
        shards, mesh=fine, in_specs=in_specs, out_specs=P(CTX, head), check_vma=False
    )
```

```python
import itertools
import math

import jax
import jax.numpy as jnp
from jax import lax
from jax.experimental import pallas as pl
from jax.experimental.pallas import tpu as pltpu
from jax.sharding import Mesh, PartitionSpec as P

QL = 1536
KVL = 512
NOPE = 128
ROPE = 64
VDIM = 128
HEADS = 4
TOK = 128
QD = NOPE + ROPE
KROWS = KVL + ROPE + 16
QROWS = HEADS * QD + 16
OROWS = HEADS * VDIM + 16

softmax_scale = 0.135
scale = softmax_scale * math.log2(math.e)
rope_base = 10000.0
masked = -1e30
floor = -1e29

F32 = jnp.float32
BF16 = jnp.bfloat16
CTX = ("za", "zb", "xl", "core")
NEAR = ("xl", "core")
VMEM = pl.BlockSpec(memory_space=pltpu.VMEM)
LIMIT = 56 * 1024 * 1024


def dot(a, b):
    return jnp.dot(a, b, preferred_element_type=F32)


def kernel_call(body, shapes, args, scratch=(), flops=0, specs=None):
    single = isinstance(shapes, tuple)
    outs = [jax.ShapeDtypeStruct(shape, BF16) for shape in ([shapes] if single else shapes)]
    return pl.pallas_call(
        body,
        out_shape=outs[0] if single else outs,
        in_specs=specs or [VMEM] * len(args),
        out_specs=VMEM if single else [VMEM] * len(outs),
        scratch_shapes=list(scratch),
        compiler_params=pltpu.CompilerParams(vmem_limit_bytes=LIMIT),
        cost_estimate=pl.CostEstimate(flops=flops, bytes_accessed=4_000_000, transcendentals=0),
    )(*args)


def position_rows(pos):
    row = lax.broadcasted_iota(jnp.int32, (16, TOK), 0)
    pos = jnp.broadcast_to(pos, (16, TOK))
    return jnp.where(row == 0, pos >> 6, jnp.where(row == 1, pos & 63, 0)).astype(F32).astype(BF16)


def pack_body(latent, pos, out):
    out[: KVL + ROPE, :] = latent[...]
    out[KVL + ROPE :, :] = position_rows(pos[...])


def weights_body(w, w_key, w_value_t):
    for h in range(HEADS):
        base = h * (NOPE + VDIM)
        cols = slice(h * NOPE, (h + 1) * NOPE)
        w_key[:, cols] = w[:, base : base + NOPE]
        w_value_t[cols, :] = w[:, base + NOPE : base + NOPE + VDIM].T


def query_body(latent, weights, cosine, sine, pos, out):
    query = dot(latent[...].T, weights[...]).T
    cos, sin = cosine[...], sine[...]
    half = ROPE // 2
    for h in range(HEADS):
        base = h * QD
        out[base : base + NOPE, :] = query[base : base + NOPE].astype(BF16)
        a = query[base + NOPE : base + NOPE + half]
        b = query[base + NOPE + half : base + QD]
        out[base + NOPE : base + QD, :] = jnp.concatenate(
            [a * cos - b * sin, a * sin + b * cos], axis=0
        ).astype(BF16)
    out[HEADS * QD :, :] = position_rows(pos[...])


def attend_body(queries, keys, w_key, w_value_t, out, latent, rope_keys, key_pos, key_cat, value_t):
    blocks = keys.shape[0]
    tokens = queries.shape[0]
    for z in range(blocks):
        rows = slice(z * TOK, (z + 1) * TOK)
        latent[rows, :] = keys[z, :KVL, :].T
        tail = keys[z, KVL:, :].astype(F32).T
        rope_keys[rows, :] = tail[:, :ROPE].astype(BF16)
        key_pos[rows, :] = tail[:, ROPE : ROPE + 1] * 64.0 + tail[:, ROPE + 1 : ROPE + 2]
        value_t[:, rows] = dot(w_value_t[...], keys[z, :KVL, :]).astype(BF16)
    expanded = dot(latent[...], w_key[...]).astype(BF16)
    for h in range(HEADS):
        key_cat[h, :, :NOPE] = expanded[:, h * NOPE : (h + 1) * NOPE]
        key_cat[h, :, NOPE:] = rope_keys[...]
    positions = key_pos[...]
    for pair in range(tokens // 2):
        two = (2 * pair, 2 * pair + 1)
        q_pos = jnp.concatenate(
            [queries[t, HEADS * QD : HEADS * QD + 2, :].astype(F32) for t in two], axis=1
        )
        q_pos = q_pos[0:1] * 64.0 + q_pos[1:2]
        visible = positions <= q_pos
        stats = []
        for h in range(HEADS):
            q = jnp.concatenate([queries[t, h * QD : (h + 1) * QD, :] for t in two], axis=1)
            scores = jnp.where(visible, dot(key_cat[h], q) * scale, masked)
            largest = jnp.maximum(jnp.max(scores, axis=0, keepdims=True), floor)
            weights = jnp.exp2(scores - largest)
            total = jnp.sum(weights, axis=0, keepdims=True)
            some = total > 0.0
            safe = jnp.where(some, total, 1.0)
            summed = dot(value_t[h * VDIM : (h + 1) * VDIM, :], weights.astype(BF16)) / safe
            level = jnp.where(some, largest + jnp.log2(safe), masked)
            first = level.astype(BF16)
            rest = level - first.astype(F32)
            second = rest.astype(BF16)
            third = (rest - second.astype(F32)).astype(BF16)
            stats += [first.astype(F32), second.astype(F32), third.astype(F32)]
            summed = summed.astype(BF16)
            for i, t in enumerate(two):
                out[t, h * VDIM : (h + 1) * VDIM, :] = summed[:, i * TOK : (i + 1) * TOK]
        stats = jnp.concatenate(stats + [jnp.zeros_like(stats[0])] * 4, axis=0).astype(BF16)
        for i, t in enumerate(two):
            out[t, HEADS * VDIM :, :] = stats[:, i * TOK : (i + 1) * TOK]


def merge_body(parts, out):
    count = parts.shape[0]
    tails = [parts[s, HEADS * VDIM :, :].astype(F32) for s in range(count)]
    for h in range(HEADS):
        levels = [t[3 * h : 3 * h + 1] + t[3 * h + 1 : 3 * h + 2] + t[3 * h + 2 : 3 * h + 3] for t in tails]
        top = levels[0]
        for level in levels[1:]:
            top = jnp.maximum(top, level)
        shares = [jnp.exp2(level - top) for level in levels]
        rows = slice(h * VDIM, (h + 1) * VDIM)
        whole = sum(shares)
        added = sum(parts[s, rows, :].astype(F32) * shares[s] for s in range(count))
        out[rows, :] = (added / whole).astype(BF16)


def project_body(w, mine, theirs, place, out, total):
    step = pl.program_id(0)
    rows = w.shape[0] * w.shape[2]
    added = 0.0
    for g in range(w.shape[1]):
        group = place[0] ^ (step * w.shape[1] + g)
        tokens = jnp.concatenate([x[2 * group + t] for x in (mine, theirs) for t in range(2)], axis=1)
        added = added + dot(w[:, g].reshape(rows, w.shape[3]), tokens)

    @pl.when(step == 0)
    def _():
        total[...] = added

    @pl.when(step > 0)
    def _():
        total[...] += added

    @pl.when(step == pl.num_programs(0) - 1)
    def _():
        here = place[1]
        tile = w.shape[2]
        for z in range(w.shape[0]):
            piece = total[z * tile : (z + 1) * tile, :].astype(BF16)
            for t in range(2):
                near, far = t * TOK, (t + 2) * TOK
                out[z % 4, here, z // 4, t] = piece[:, near : near + TOK]
                out[z % 4, 1 - here, z // 4, t] = piece[:, far : far + TOK]


def project(w, mine, theirs, place):
    tiles, groups, rows, depth = w.shape
    wide = 4 * TOK
    return pl.pallas_call(
        project_body,
        grid=(groups // 2,),
        out_shape=jax.ShapeDtypeStruct((tiles // 2, 2, 2, 2, rows, TOK), BF16),
        in_specs=[
            pl.BlockSpec((tiles, 2, rows, depth), lambda i: (0, i, 0, 0)),
            pl.BlockSpec(mine.shape, lambda i: (0, 0, 0)),
            pl.BlockSpec(mine.shape, lambda i: (0, 0, 0)),
            pl.BlockSpec(memory_space=pltpu.SMEM),
        ],
        out_specs=pl.BlockSpec((tiles // 2, 2, 2, 2, rows, TOK), lambda i: (0, 0, 0, 0, 0, 0)),
        scratch_shapes=[pltpu.VMEM((tiles * rows, wide), F32)],
        compiler_params=pltpu.CompilerParams(vmem_limit_bytes=LIMIT),
        cost_estimate=pl.CostEstimate(
            flops=2 * groups * tiles * rows * depth * wide, bytes_accessed=5_000_000, transcendentals=0
        ),
    )(w, mine, theirs, place)


def sent_to_all(array, axis):
    copies = jnp.broadcast_to(array, (lax.axis_size(axis), *array.shape))
    return lax.all_to_all(copies, axis, split_axis=0, concat_axis=0, tiled=True)


def crossed(half, flip):
    pairs = []
    for b, c, d in itertools.product(range(2), repeat=3):
        pairs.append(((b * 2 + c) * 2 + d, ((d ^ flip) * 2 + (c ^ half)) * 2 + b))
    return pairs


def shards(q_latent, latent_cache, w_q_up, w_kv_up, w_out, token_pos, start_offset):
    columns = w_out.T.reshape(4, -1, HEADS * VDIM)
    part = columns.shape[1]
    yl = lax.axis_index("yl")
    xh = lax.axis_index("xh")
    w_mine = [
        lax.ppermute(
            lax.dynamic_index_in_dim(columns, (xh ^ half) * 2 + (yl ^ flip), 0, keepdims=False),
            ("xl", "xh", "yl"),
            crossed(half, flip),
        )
        for flip in range(2)
        for half in range(2)
    ]
    keys = kernel_call(pack_body, (KROWS, TOK), (latent_cache.T, token_pos[None]))
    keys = lax.all_gather(keys, ("za", "zb"), axis=0, tiled=False)
    latent = sent_to_all(q_latent.T, ("xh", "yh", "yl")).reshape(QL, TOK)

    absolute = (token_pos + start_offset[0]).astype(F32)
    freqs = rope_base ** (-jnp.arange(ROPE // 2, dtype=F32) * 2.0 / ROPE)
    angle = freqs[:, None] * absolute[None, :]
    query = kernel_call(
        query_body,
        (QROWS, TOK),
        (latent, w_q_up, jnp.cos(angle), jnp.sin(angle), token_pos[None]),
        flops=300_000_000,
    )
    query, w_mine = lax.optimization_barrier((query, w_mine))
    w_four = jnp.pad(jnp.stack(w_mine), ((0, 0), (0, -part % 16), (0, 0)))
    w_all = lax.all_gather(w_four, ("za", "zb"), axis=0, tiled=False)
    queries = lax.all_gather(query, NEAR, axis=0, tiled=False)

    w_key, w_value_t = kernel_call(weights_body, [(KVL, HEADS * NOPE), (HEADS * VDIM, KVL)], (w_kv_up,))
    count = keys.shape[0] * TOK
    parts = kernel_call(
        attend_body,
        (4, OROWS, TOK),
        (queries, keys, w_key, w_value_t),
        scratch=(
            pltpu.VMEM((count, KVL), BF16),
            pltpu.VMEM((count, ROPE), BF16),
            pltpu.VMEM((count, 1), F32),
            pltpu.VMEM((HEADS, count, QD), BF16),
            pltpu.VMEM((HEADS * VDIM, count), BF16),
        ),
        flops=3_500_000_000,
    )
    parts = lax.all_to_all(parts, NEAR, split_axis=0, concat_axis=0, tiled=True)
    mine = kernel_call(merge_body, (HEADS * VDIM, TOK), (parts,), flops=1_000_000)
    mine = sent_to_all(mine, ("yl", "xh", "xl"))
    theirs = lax.ppermute(mine, "core", [(0, 1), (1, 0)])
    place = jnp.stack([lax.axis_index("xl") * 2 + xh, lax.axis_index("core")]).astype(jnp.int32)
    partial = project(w_all, mine, theirs, place)
    partial = partial.reshape(32, -1, TOK)
    arrived = lax.all_to_all(partial, ("yh", "core", "xh", "xl"), split_axis=0, concat_axis=0, tiled=True)
    arrived = arrived.reshape(4, 8, -1, TOK)[:, :, :part]
    return arrived.astype(F32).sum(axis=0).astype(BF16).reshape(-1, TOK).T


def solution(mesh):
    fine = Mesh(mesh.devices.reshape(2, 4, 2, 2, 2, 4, 2), ("za", "zb", "xl", "core", "xh", "yh", "yl"))
    head = ("xh", "yh", "yl")
    in_specs = (
        P(CTX, head),
        P(CTX, None),
        P(None, head),
        P(None, head),
        P(head, CTX),
        P(CTX),
        P(),
    )
    return jax.shard_map(
        shards, mesh=fine, in_specs=in_specs, out_specs=P(CTX, head), check_vma=False
    )
```

```python
import itertools
import math

import jax
import jax.numpy as jnp
from jax import lax
from jax.experimental import pallas as pl
from jax.experimental.pallas import tpu as pltpu
from jax.sharding import Mesh, PartitionSpec as P

QL = 1536
KVL = 512
NOPE = 128
ROPE = 64
VDIM = 128
HEADS = 4
TOK = 128
QD = NOPE + ROPE
KROWS = KVL + ROPE + 16
QROWS = HEADS * QD + 16
OROWS = HEADS * VDIM + 16

softmax_scale = 0.135
scale = softmax_scale * math.log2(math.e)
rope_base = 10000.0
masked = -1e30
floor = -1e29

F32 = jnp.float32
BF16 = jnp.bfloat16
CTX = ("za", "zb", "xl", "core")
NEAR = ("xl", "core")
VMEM = pl.BlockSpec(memory_space=pltpu.VMEM)
LIMIT = 56 * 1024 * 1024


def dot(a, b):
    return jnp.dot(a, b, preferred_element_type=F32)


def kernel_call(body, shapes, args, scratch=(), flops=0, specs=None):
    single = isinstance(shapes, tuple)
    outs = [jax.ShapeDtypeStruct(shape, BF16) for shape in ([shapes] if single else shapes)]
    return pl.pallas_call(
        body,
        out_shape=outs[0] if single else outs,
        in_specs=specs or [VMEM] * len(args),
        out_specs=VMEM if single else [VMEM] * len(outs),
        scratch_shapes=list(scratch),
        compiler_params=pltpu.CompilerParams(vmem_limit_bytes=LIMIT),
        cost_estimate=pl.CostEstimate(flops=flops, bytes_accessed=4_000_000, transcendentals=0),
    )(*args)


def position_rows(pos):
    row = lax.broadcasted_iota(jnp.int32, (16, TOK), 0)
    pos = jnp.broadcast_to(pos, (16, TOK))
    return jnp.where(row == 0, pos >> 6, jnp.where(row == 1, pos & 63, 0)).astype(F32).astype(BF16)


def pack_body(latent, pos, out):
    out[: KVL + ROPE, :] = latent[...]
    out[KVL + ROPE :, :] = position_rows(pos[...])


def weights_body(w, w_key, w_value_t):
    for h in range(HEADS):
        base = h * (NOPE + VDIM)
        cols = slice(h * NOPE, (h + 1) * NOPE)
        w_key[:, cols] = w[:, base : base + NOPE]
        w_value_t[cols, :] = w[:, base + NOPE : base + NOPE + VDIM].T


def query_body(latent, weights, cosine, sine, pos, out):
    query = dot(latent[...].T, weights[...]).T
    cos, sin = cosine[...], sine[...]
    half = ROPE // 2
    for h in range(HEADS):
        base = h * QD
        out[base : base + NOPE, :] = query[base : base + NOPE].astype(BF16)
        a = query[base + NOPE : base + NOPE + half]
        b = query[base + NOPE + half : base + QD]
        out[base + NOPE : base + QD, :] = jnp.concatenate(
            [a * cos - b * sin, a * sin + b * cos], axis=0
        ).astype(BF16)
    out[HEADS * QD :, :] = position_rows(pos[...])


def attend_body(queries, keys, w_key, w_value_t, out, latent, rope_keys, key_pos, key_cat, value_t):
    blocks = keys.shape[0]
    tokens = queries.shape[0]
    for z in range(blocks):
        rows = slice(z * TOK, (z + 1) * TOK)
        latent[rows, :] = keys[z, :KVL, :].T
        tail = keys[z, KVL:, :].astype(F32).T
        rope_keys[rows, :] = tail[:, :ROPE].astype(BF16)
        key_pos[rows, :] = tail[:, ROPE : ROPE + 1] * 64.0 + tail[:, ROPE + 1 : ROPE + 2]
        value_t[:, rows] = dot(w_value_t[...], keys[z, :KVL, :]).astype(BF16)
    expanded = dot(latent[...], w_key[...]).astype(BF16)
    for h in range(HEADS):
        key_cat[h, :, :NOPE] = expanded[:, h * NOPE : (h + 1) * NOPE]
        key_cat[h, :, NOPE:] = rope_keys[...]
    positions = key_pos[...]
    q_pos = jnp.concatenate(
        [queries[t, HEADS * QD : HEADS * QD + 2, :].astype(F32) for t in range(tokens)], axis=1
    )
    q_pos = q_pos[0:1] * 64.0 + q_pos[1:2]
    stats = []
    visible = positions <= q_pos
    for h in range(HEADS):
        q = jnp.concatenate([queries[t, h * QD : (h + 1) * QD, :] for t in range(tokens)], axis=1)
        scores = jnp.where(visible, dot(key_cat[h], q) * scale, masked)
        largest = jnp.maximum(jnp.max(scores, axis=0, keepdims=True), floor)
        weights = jnp.exp2(scores - largest)
        total = jnp.sum(weights, axis=0, keepdims=True)
        some = total > 0.0
        safe = jnp.where(some, total, 1.0)
        summed = dot(value_t[h * VDIM : (h + 1) * VDIM, :], weights.astype(BF16)) * (1.0 / safe)
        level = jnp.where(some, largest + jnp.log2(safe), masked)
        first = level.astype(BF16)
        rest = level - first.astype(F32)
        second = rest.astype(BF16)
        third = (rest - second.astype(F32)).astype(BF16)
        stats += [first.astype(F32), second.astype(F32), third.astype(F32)]
        summed = summed.astype(BF16)
        for t in range(tokens):
            out[t, h * VDIM : (h + 1) * VDIM, :] = summed[:, t * TOK : (t + 1) * TOK]
    stats = jnp.concatenate(stats + [jnp.zeros_like(stats[0])] * 4, axis=0).astype(BF16)
    for t in range(tokens):
        out[t, HEADS * VDIM :, :] = stats[:, t * TOK : (t + 1) * TOK]


def merge_body(parts, out):
    count = parts.shape[0]
    tails = [parts[s, HEADS * VDIM :, :].astype(F32) for s in range(count)]
    for h in range(HEADS):
        levels = [t[3 * h : 3 * h + 1] + t[3 * h + 1 : 3 * h + 2] + t[3 * h + 2 : 3 * h + 3] for t in tails]
        top = levels[0]
        for level in levels[1:]:
            top = jnp.maximum(top, level)
        shares = [jnp.exp2(level - top) for level in levels]
        rows = slice(h * VDIM, (h + 1) * VDIM)
        whole = sum(shares)
        added = sum(parts[s, rows, :].astype(F32) * shares[s] for s in range(count))
        out[rows, :] = (added / whole).astype(BF16)


def project_body(w, mine, theirs, place, out, total):
    step = pl.program_id(0)
    rows = w.shape[0] * w.shape[2]
    added = 0.0
    for g in range(w.shape[1]):
        group = place[0] ^ (step * w.shape[1] + g)
        tokens = jnp.concatenate([x[2 * group + t] for x in (mine, theirs) for t in range(2)], axis=1)
        added = added + dot(w[:, g].reshape(rows, w.shape[3]), tokens)

    @pl.when(step == 0)
    def _():
        total[...] = added

    @pl.when(step > 0)
    def _():
        total[...] += added

    @pl.when(step == pl.num_programs(0) - 1)
    def _():
        here = place[1]
        tile = w.shape[2]
        for z in range(w.shape[0]):
            piece = total[z * tile : (z + 1) * tile, :].astype(BF16)
            for t in range(2):
                near, far = t * TOK, (t + 2) * TOK
                out[z % 4, here, z // 4, t] = piece[:, near : near + TOK]
                out[z % 4, 1 - here, z // 4, t] = piece[:, far : far + TOK]


def project(w, mine, theirs, place):
    tiles, groups, rows, depth = w.shape
    wide = 4 * TOK
    return pl.pallas_call(
        project_body,
        grid=(groups // 2,),
        out_shape=jax.ShapeDtypeStruct((tiles // 2, 2, 2, 2, rows, TOK), BF16),
        in_specs=[
            pl.BlockSpec((tiles, 2, rows, depth), lambda i: (0, i, 0, 0)),
            pl.BlockSpec(mine.shape, lambda i: (0, 0, 0)),
            pl.BlockSpec(mine.shape, lambda i: (0, 0, 0)),
            pl.BlockSpec(memory_space=pltpu.SMEM),
        ],
        out_specs=pl.BlockSpec((tiles // 2, 2, 2, 2, rows, TOK), lambda i: (0, 0, 0, 0, 0, 0)),
        scratch_shapes=[pltpu.VMEM((tiles * rows, wide), F32)],
        compiler_params=pltpu.CompilerParams(vmem_limit_bytes=LIMIT),
        cost_estimate=pl.CostEstimate(
            flops=2 * groups * tiles * rows * depth * wide, bytes_accessed=5_000_000, transcendentals=0
        ),
    )(w, mine, theirs, place)


def sent_to_all(array, axis):
    copies = jnp.broadcast_to(array, (lax.axis_size(axis), *array.shape))
    return lax.all_to_all(copies, axis, split_axis=0, concat_axis=0, tiled=True)


def crossed(half, flip):
    pairs = []
    for b, c, d in itertools.product(range(2), repeat=3):
        pairs.append(((b * 2 + c) * 2 + d, ((d ^ flip) * 2 + (c ^ half)) * 2 + b))
    return pairs


def shards(q_latent, latent_cache, w_q_up, w_kv_up, w_out, token_pos, start_offset):
    columns = w_out.T.reshape(4, -1, HEADS * VDIM)
    part = columns.shape[1]
    yl = lax.axis_index("yl")
    xh = lax.axis_index("xh")
    w_mine = [
        lax.ppermute(
            lax.dynamic_index_in_dim(columns, (xh ^ half) * 2 + (yl ^ flip), 0, keepdims=False),
            ("xl", "xh", "yl"),
            crossed(half, flip),
        )
        for flip in range(2)
        for half in range(2)
    ]
    keys = kernel_call(pack_body, (KROWS, TOK), (latent_cache.T, token_pos[None]))
    keys = lax.all_gather(keys, ("za", "zb"), axis=0, tiled=False)
    latent = sent_to_all(q_latent.T, ("xh", "yh", "yl")).reshape(QL, TOK)

    absolute = (token_pos + start_offset[0]).astype(F32)
    freqs = rope_base ** (-jnp.arange(ROPE // 2, dtype=F32) * 2.0 / ROPE)
    angle = freqs[:, None] * absolute[None, :]
    query = kernel_call(
        query_body,
        (QROWS, TOK),
        (latent, w_q_up, jnp.cos(angle), jnp.sin(angle), token_pos[None]),
        flops=300_000_000,
    )
    query, w_mine = lax.optimization_barrier((query, w_mine))
    w_four = jnp.pad(jnp.stack(w_mine), ((0, 0), (0, -part % 16), (0, 0)))
    w_all = lax.all_gather(w_four, ("za", "zb"), axis=0, tiled=False)
    queries = lax.all_gather(query, NEAR, axis=0, tiled=False)

    w_key, w_value_t = kernel_call(weights_body, [(KVL, HEADS * NOPE), (HEADS * VDIM, KVL)], (w_kv_up,))
    count = keys.shape[0] * TOK
    parts = kernel_call(
        attend_body,
        (4, OROWS, TOK),
        (queries, keys, w_key, w_value_t),
        scratch=(
            pltpu.VMEM((count, KVL), BF16),
            pltpu.VMEM((count, ROPE), BF16),
            pltpu.VMEM((count, 1), F32),
            pltpu.VMEM((HEADS, count, QD), BF16),
            pltpu.VMEM((HEADS * VDIM, count), BF16),
        ),
        flops=3_500_000_000,
    )
    parts = lax.all_to_all(parts, NEAR, split_axis=0, concat_axis=0, tiled=True)
    mine = kernel_call(merge_body, (HEADS * VDIM, TOK), (parts,), flops=1_000_000)
    mine = sent_to_all(mine, ("yl", "xh", "xl"))
    theirs = lax.ppermute(mine, "core", [(0, 1), (1, 0)])
    place = jnp.stack([lax.axis_index("xl") * 2 + xh, lax.axis_index("core")]).astype(jnp.int32)
    partial = project(w_all, mine, theirs, place)
    partial = partial.reshape(32, -1, TOK)
    arrived = lax.all_to_all(partial, ("yh", "core", "xh", "xl"), split_axis=0, concat_axis=0, tiled=True)
    arrived = arrived.reshape(4, 8, -1, TOK)[:, :, :part]
    return arrived.astype(F32).sum(axis=0).astype(BF16).reshape(-1, TOK).T


def solution(mesh):
    fine = Mesh(mesh.devices.reshape(2, 4, 2, 2, 2, 4, 2), ("za", "zb", "xl", "core", "xh", "yh", "yl"))
    head = ("xh", "yh", "yl")
    in_specs = (
        P(CTX, head),
        P(CTX, None),
        P(None, head),
        P(None, head),
        P(head, CTX),
        P(CTX),
        P(),
    )
    return jax.shard_map(
        shards, mesh=fine, in_specs=in_specs, out_specs=P(CTX, head), check_vma=False
    )
```
